32 devices in a mesh: section: 2 (over core), ctx: 16 (over z, y, x).
Axes of the slice: x: 2, y: 2, z: 4, core: 2. Of those that a mesh axis runs over, the one named last changes fastest.
Arguments:
- projected: bfloat16 [2, 2048, 3, 2048], P('section', 'ctx'), may hold values from -6 to 6
- feat_taps: bfloat16 [2, 3, 3, 2048], P('section'), may hold values from -3 to 3
- skip_gain: float32 [2, 2048], P('section'), may hold values from -3 to 3
- long_filter: bfloat16 [2, 2048, 2048], P('section', 'ctx'), may hold values from -4 to 4
Outputs:
- handed: bfloat16 [2, 2048, 2048], P('section', 'ctx')
The draws below stay inside these ranges and needn't reach their ends.
All inputs are finite; a program needn't handle non-finite values.
Results may differ from the reference program's by a relative error of at most 0.0068.
Values may be sent and summed in bfloat16 or wider, within the bound.
A program may use at most 128 MiB of HBM per device.

```python
import math
import jax
import jax.numpy as jnp
from jax import lax

L = 128
C = 2048
FEAT = 3
SECTIONS = 2
SEQ = 2048
N_CTX = 16


def draw_long_filter(key, part):
    key_noise = jax.random.fold_in(key, 11)
    key_decay = jax.random.fold_in(key, 12)
    positions = jnp.arange(SEQ).astype(jnp.float32)
    decay = jnp.exp(jax.random.uniform(key_decay, (SECTIONS, 1, C), jnp.float32, math.log(0.2), math.log(3.0)))
    envelope = jnp.exp(-decay * positions[None, :, None] / SEQ)
    base = math.sqrt(2.0 / SEQ)
    noise = jax.random.normal(key_noise, (SECTIONS, SEQ, C), jnp.float32)
    values = base * envelope * noise
    return jnp.clip(values, -4.0, 4.0).astype(jnp.bfloat16)


def levels(stream_key, shape, split, low, top_value):
    gain, own = 1.0, jax.random.fold_in(stream_key, 6)
    for axis_at, parts in split:
        heights = jnp.exp(jax.random.uniform(jax.random.fold_in(own, axis_at), (parts,), jnp.float32, low / len(split), top_value / len(split)))
        gain = gain * jnp.repeat(heights, shape[axis_at] // parts).reshape([-1 if axis == axis_at else 1 for axis in range(len(shape))])
    return gain


def centred(stream_key, shape, spread, most, pieces=(), dtype=jnp.bfloat16):
    entries = spread * jax.random.normal(stream_key, shape, jnp.float32)
    if pieces:
        entries = entries * levels(stream_key, shape, pieces, -0.22, 0.18)
    return jnp.clip(entries, -most, most).astype(dtype)


def setup_inputs(seed: int = 0) -> dict:
    seeds = jax.random.split(jax.random.key(seed), 5)
    projected = centred(seeds[0], (SECTIONS, SEQ, 3, C), 1.0, 6.0, ((0, 2), (1, 16)))
    feat_taps = centred(seeds[1], (SECTIONS, FEAT, 3, C), 0.6, 3.0, ((0, 2),))
    skip_gain = centred(seeds[2], (SECTIONS, C), 0.5, 3.0, ((0, 2),), jnp.float32)
    long_filter = draw_long_filter(jax.random.fold_in(seeds[4], 71), 0)
    return {"projected": projected, "feat_taps": feat_taps, "skip_gain": skip_gain, "long_filter": long_filter}


def phase_table(first_ids, second_ids, modulus, orient):
    whole = (first_ids[:, None] * second_ids[None, :]) % modulus
    return orient * 2.0 * math.pi * whole.astype(jnp.float32) / modulus


def complex_einsum(joined, mat_re, mat_im, val_re, val_im):
    table = jnp.stack([jnp.stack([mat_re, -mat_im]), jnp.stack([mat_im, mat_re])])
    values = jnp.stack([val_re, val_im])
    combined = jnp.einsum(joined, table, values, precision=lax.Precision.HIGHEST)
    return combined[0], combined[1]


def rotate(val_re, val_im, angles):
    cosine = jnp.cos(angles)
    sine_part = jnp.sin(angles)
    return cosine * val_re - sine_part * val_im, cosine * val_im + sine_part * val_re


def rounded(values):
    return lax.optimization_barrier(values.astype(jnp.bfloat16)).astype(jnp.float32)


def reference(projected, feat_taps, skip_gain, long_filter):
    devices = N_CTX
    sequence = SEQ
    length = L
    halfwidth = C // 2
    bin_index = jnp.arange(2 * devices).astype(jnp.int32)
    block_index = jnp.arange(devices).astype(jnp.int32)
    column_index = jnp.arange(length).astype(jnp.int32)
    forward_phase = phase_table(bin_index, block_index, 2 * devices, -1.0)
    forward_twist = phase_table(bin_index, column_index, 2 * sequence, -1.0)
    inverse_twist = phase_table(bin_index, column_index, 2 * sequence, 1.0)
    inverse_phase = phase_table(block_index, bin_index, 2 * devices, 1.0)

    def one_section(section_inputs):
        inputs, taps, skip_row, filter_taps = section_inputs
        extended = jnp.concatenate([jnp.zeros((FEAT - 1, 3, C), jnp.float32), inputs.astype(jnp.float32)], axis=0)
        featured = jnp.zeros((sequence, 3, C), jnp.float32)
        for offset in range(FEAT):
            featured = featured + taps[offset].astype(jnp.float32) * extended[FEAT - 1 - offset:FEAT - 1 - offset + sequence]
        query_part = featured[:, 0]
        gated_input = featured[:, 1] * featured[:, 2]
        packed = jnp.stack([rounded(gated_input), filter_taps.astype(jnp.float32)]).reshape(2, devices, length, C)
        part_re, part_im = complex_einsum("yzrp,zkpjh->ykrjh", jnp.cos(forward_phase), jnp.sin(forward_phase), packed[..., :halfwidth], packed[..., halfwidth:])
        part_re, part_im = rotate(part_re, part_im, forward_twist[None, :, :, None])
        part_re = rounded(part_re)
        part_im = rounded(part_im)
        spectrum = jnp.fft.fft(lax.complex(part_re, part_im), axis=2)
        mirror = jnp.flip(jnp.roll(jnp.flip(spectrum, 1), 1, 1), 2)
        mirror = jnp.where((bin_index == 0)[None, :, None, None], jnp.roll(mirror, 1, 2), mirror)
        conj_mirror = jnp.conj(mirror)
        first_part = (spectrum + conj_mirror) / 2
        second_part = (spectrum - conj_mirror) * (-0.5j)
        product = first_part[0] * first_part[1] + 1j * (second_part[0] * second_part[1])
        restored = jnp.fft.ifft(product, axis=1) * length
        rest_re, rest_im = rotate(jnp.real(restored), jnp.imag(restored), inverse_twist[:, :, None])
        rest_re = rounded(rest_re)
        rest_im = rounded(rest_im)
        conv_re, conv_im = complex_einsum("yzpr,zrjh->ypjh", jnp.cos(inverse_phase), jnp.sin(inverse_phase), rest_re, rest_im)
        convolved = rounded(jnp.concatenate([conv_re, conv_im], axis=-1) / (2 * sequence)).reshape(sequence, C)
        return (query_part * (convolved + skip_row * gated_input)).astype(jnp.bfloat16)

    mixers = lax.map(one_section, (projected, feat_taps, skip_gain, long_filter))
    return jnp.roll(mixers, 1, axis=0)
```

```python
import functools
import math

import jax
import jax.numpy as jnp
import ml_dtypes
import numpy as np
from jax import lax
from jax.experimental import pallas as pl
from jax.experimental.pallas import tpu as pltpu
from jax.sharding import PartitionSpec as P

GROUP = 16
MESH = pl.DeviceIdType.MESH


def tables(devices, length):
    total = devices * length
    r = np.arange(devices)
    p = np.arange(devices)
    s = np.arange(length)
    j = np.arange(length)
    short = np.exp(2j * np.pi * (((1 + 4 * r[:, None]) * p[None, :]) % (4 * devices)) / (4 * devices))
    phase = ((1 + 4 * r[:, None, None]) * j[None, None, :] + 4 * devices * s[None, :, None] * j[None, None, :]) % (4 * total)
    long = np.exp(2j * np.pi * phase / (4 * total))
    forward = np.concatenate(
        [np.concatenate([long.real, -long.imag], 2), np.concatenate([long.imag, long.real], 2)], 1
    )
    parts = np.stack([short.real, short.imag])
    return parts, forward


def two_terms(values):
    high = values.astype(ml_dtypes.bfloat16)
    low = (values - high.astype(np.float64)).astype(ml_dtypes.bfloat16)
    return high, low


def body_plain(projected, feat_taps, skip_gain, long_filter):
    devices = lax.axis_size("ctx")
    sections = lax.axis_size("section")
    streams = projected[0]
    length, _, channels = streams.shape
    share = channels // devices
    feat_count = feat_taps.shape[1]
    earlier = lax.ppermute(
        streams[length - (feat_count - 1) :], "ctx", [(i, i + 1) for i in range(devices - 1)]
    )
    extended = jnp.concatenate([earlier, streams], axis=0).astype(jnp.float32)
    featured = jnp.zeros((length, 3, channels), jnp.float32)
    for offset in range(feat_count):
        first = feat_count - 1 - offset
        featured = featured + feat_taps[0, offset].astype(jnp.float32) * extended[first : first + length]
    query = featured[:, 0]
    gated = featured[:, 1] * featured[:, 2]
    packed = jnp.stack([gated.astype(jnp.bfloat16), long_filter[0]])
    packed = packed.reshape(2, length, devices, share).transpose(2, 0, 1, 3)
    arrived = lax.all_to_all(packed, "ctx", split_axis=0, concat_axis=0, tiled=True)
    parts, forward = tables(devices, length)
    parts = jnp.asarray(parts, jnp.float32)
    forward = jnp.asarray(forward, jnp.float32)
    high = lax.Precision.HIGHEST
    blocks = arrived.astype(jnp.float32)
    partial = jnp.einsum("qrp,pkjc->krqjc", parts, blocks, precision=high)
    partial = partial.reshape(2, devices, 2 * length, share)
    spectrum = jnp.einsum("rxy,kryc->krxc", forward, partial, precision=high)
    data_re, data_im = spectrum[0, :, :length], spectrum[0, :, length:]
    filt_re, filt_im = spectrum[1, :, :length], spectrum[1, :, length:]
    product = jnp.concatenate(
        [data_re * filt_re - data_im * filt_im, data_re * filt_im + data_im * filt_re], 1
    )
    restored = jnp.einsum("rxy,rxc->ryc", forward, product, precision=high)
    restored = restored.reshape(devices, 2, length, share)
    conv = jnp.einsum("qrp,rqjc->pjc", parts, restored, precision=high) / (devices * length)
    back = lax.all_to_all(conv.astype(jnp.bfloat16), "ctx", split_axis=0, concat_axis=0, tiled=True)
    convolved = back.transpose(1, 0, 2).reshape(length, channels).astype(jnp.float32)
    output = (query * (convolved + skip_gain[0] * gated)).astype(jnp.bfloat16)
    return lax.ppermute(
        output[None], "section", [(i, (i + 1) % sections) for i in range(sections)]
    )


def partner(me, step, devices, arriving=False):
    if devices & (devices - 1) == 0:
        return me ^ step
    return lax.rem(me + (devices - step if arriving else step), devices)


def kernel(
    devices,
    sections,
    streams_ref,
    taps_ref,
    skip_ref,
    filter_ref,
    short_ref,
    back_ref,
    long_ref,
    longback_ref,
    out_ref,
    streams,
    short,
    back,
    long,
    longback,
    tail,
    halo,
    gated_out,
    query,
    skipped,
    filter_in,
    gated_in,
    query_in,
    skipped_in,
    partial,
    spectrum,
    restored,
    conv,
    conv_in,
    local_sem,
    halo_sem,
    filter_send,
    filter_recv,
    gated_send,
    gated_recv,
    cross_sem,
    conv_send,
    conv_recv,
):
    me = lax.axis_index("ctx")
    beyond = lax.rem(lax.axis_index("section") + 1, sections)
    length, channels = filter_ref.shape
    share = channels // devices
    feat_count = taps_ref.shape[0] // 3
    keep = feat_count - 1
    rows = devices * GROUP

    def lanes(index):
        return pl.ds(pl.multiple_of(index * share, share), share)

    def filter_copy(step):
        to = partner(me, step, devices)
        return pltpu.make_async_remote_copy(
            src_ref=filter_ref.at[:, lanes(to)],
            dst_ref=filter_in.at[me],
            send_sem=filter_send.at[step],
            recv_sem=filter_recv.at[step],
            device_id={"ctx": to},
            device_id_type=MESH,
        )

    def gated_copy(step):
        to = partner(me, step, devices)
        return pltpu.make_async_remote_copy(
            src_ref=gated_out.at[to],
            dst_ref=gated_in.at[me],
            send_sem=gated_send.at[step],
            recv_sem=gated_recv.at[step],
            device_id={"ctx": to},
            device_id_type=MESH,
        )

    def conv_copy(step):
        to = partner(me, step, devices)
        return pltpu.make_async_remote_copy(
            src_ref=conv.at[to],
            dst_ref=conv_in.at[me],
            send_sem=conv_send.at[step],
            recv_sem=conv_recv.at[step],
            device_id={"ctx": to, "section": beyond},
            device_id_type=MESH,
        )

    def cross_copy(index, source, target):
        return pltpu.make_async_remote_copy(
            src_ref=source,
            dst_ref=target,
            send_sem=cross_sem.at[2 * index],
            recv_sem=cross_sem.at[2 * index + 1],
            device_id={"section": beyond},
            device_id_type=MESH,
        )

    halo_copy = pltpu.make_async_remote_copy(
        src_ref=tail,
        dst_ref=halo,
        send_sem=halo_sem.at[0],
        recv_sem=halo_sem.at[1],
        device_id={"ctx": lax.rem(me + 1, devices)},
        device_id_type=MESH,
    )
    load_streams = pltpu.make_async_copy(streams_ref, streams, local_sem.at[0])
    own_filter = pltpu.make_async_copy(filter_ref.at[:, lanes(me)], filter_in.at[me], local_sem.at[1])
    loads = [
        pltpu.make_async_copy(source, target, local_sem.at[2 + i])
        for i, (source, target) in enumerate(
            [(short_ref, short), (long_ref, long), (longback_ref, longback), (back_ref, back)]
        )
    ]

    load_streams.start()

    @pl.loop(0, devices - 1)
    def _(i):
        filter_copy(devices - 1 - i).start()

    own_filter.start()
    load_streams.wait()
    for copy in loads:
        copy.start()

    for stream in range(3):
        last = streams[stream, length - GROUP :, :].astype(jnp.float32)
        tail[stream * keep : (stream + 1) * keep, :] = last[GROUP - keep :, :]
    if tail.shape[0] > 3 * keep:
        tail[3 * keep :, :] = jnp.zeros((tail.shape[0] - 3 * keep, channels), jnp.float32)

    @pl.when(me < devices - 1)
    def _():
        halo_copy.start()

    @pl.when(me > 0)
    def _():
        halo_copy.wait_recv()

    @pl.when(me == 0)
    def _():
        halo[...] = jnp.zeros_like(halo)

    row_ids = lax.broadcasted_iota(jnp.int32, (length, share), 0)

    def features(index):
        at = lanes(index)
        found = []
        for stream in range(3):
            values = streams[stream, :, at].astype(jnp.float32)
            total = taps_ref[pl.ds(stream, 1), at] * values
            for offset in range(1, feat_count):
                moved = pltpu.roll(values, offset, 0)
                for row in range(offset):
                    before = halo[pl.ds(stream * keep + keep - offset + row, 1), at]
                    moved = jnp.where(row_ids == row, before, moved)
                total = total + taps_ref[pl.ds(offset * 3 + stream, 1), at] * moved
            found.append(total)
        gated = found[1] * found[2]
        gated_out[index] = gated.astype(jnp.bfloat16)
        query[index] = found[0]
        skipped[index] = skip_ref[:, at] * gated

    @pl.loop(0, devices - 1)
    def _(i):
        step = devices - 1 - i
        features(partner(me, step, devices))
        gated_copy(step).start()

    features(me)
    gated_in[me] = gated_out[me]
    cross_copy(0, query, query_in).start()
    cross_copy(1, skipped, skipped_in).start()

    def short_transform(arrived):
        @pl.loop(0, length // GROUP)
        def _(g):
            at = pl.ds(pl.multiple_of(g * GROUP, GROUP), GROUP)
            values = arrived[:, at, :].reshape(rows, share)
            done = jnp.dot(short[0], values, preferred_element_type=jnp.float32)
            done = done + jnp.dot(short[1], values, preferred_element_type=jnp.float32)
            done = done.astype(jnp.bfloat16).reshape(2, devices, GROUP, share)
            partial[:, at, :] = done[0]
            partial[:, pl.ds(pl.multiple_of(length + g * GROUP, GROUP), GROUP), :] = done[1]

    own_filter.wait()

    @pl.loop(0, devices - 1)
    def _(i):
        filter_copy(devices - 1 - i).wait_recv()

    for copy in loads:
        copy.wait()
    short_transform(filter_in)

    @pl.loop(0, devices)
    def _(r):
        spectrum[r] = jnp.dot(long[r], partial[r], preferred_element_type=jnp.float32)

    @pl.loop(0, devices - 1)
    def _(i):
        gated_copy(devices - 1 - i).wait_recv()

    short_transform(gated_in)

    @pl.loop(0, devices)
    def _(r):
        data = jnp.dot(long[r], partial[r], preferred_element_type=jnp.float32)
        data_re, data_im = data[:length], data[length:]
        filt_re, filt_im = spectrum[r, :length], spectrum[r, length:]
        product = jnp.concatenate(
            [data_re * filt_re - data_im * filt_im, data_re * filt_im + data_im * filt_re], 0
        )
        restored[r] = jnp.dot(
            longback[r], product.astype(jnp.bfloat16), preferred_element_type=jnp.float32
        ).astype(jnp.bfloat16)

    @pl.loop(0, length // GROUP)
    def _(g):
        at = pl.ds(pl.multiple_of(g * GROUP, GROUP), GROUP)
        real = restored[:, at, :].reshape(rows, share)
        imag = restored[:, pl.ds(pl.multiple_of(length + g * GROUP, GROUP), GROUP), :].reshape(rows, share)
        values = jnp.concatenate([real, imag], 0)
        done = jnp.dot(back[0], values, preferred_element_type=jnp.float32)
        done = done + jnp.dot(back[1], values, preferred_element_type=jnp.float32)
        conv[:, at, :] = done.astype(jnp.bfloat16).reshape(devices, GROUP, share)

    @pl.loop(0, devices)
    def _(i):
        conv_copy(devices - 1 - i).start()

    cross_copy(0, query, query_in).wait()
    cross_copy(1, skipped, skipped_in).wait()

    @pl.when(me < devices - 1)
    def _():
        halo_copy.wait_send()

    @pl.loop(0, devices - 1)
    def _(i):
        filter_copy(devices - 1 - i).wait_send()
        gated_copy(devices - 1 - i).wait_send()

    @pl.loop(0, devices)
    def _(i):
        step = lax.rem(i, devices)
        conv_copy(step).wait_recv()
        source = partner(me, step, devices, arriving=True)
        mixed = query_in[source] * (conv_in[source].astype(jnp.float32) + skipped_in[source])
        out_ref[:, lanes(source)] = mixed.astype(jnp.bfloat16)

    @pl.loop(0, devices)
    def _(i):
        conv_copy(i).wait_send()


def body_kernel(projected, feat_taps, skip_gain, long_filter):
    devices = lax.axis_size("ctx")
    sections = lax.axis_size("section")
    streams = jnp.transpose(projected[0], (1, 0, 2))
    _, length, channels = streams.shape
    share = channels // devices
    feat_count = feat_taps.shape[1]
    taps = feat_taps[0].astype(jnp.float32).reshape(feat_count * 3, channels)
    parts, forward = tables(devices, length)
    eye = np.eye(GROUP)
    short = np.einsum("qrp,ab->qrapb", parts, eye).reshape(2 * devices * GROUP, devices * GROUP)
    short_pair = np.stack(two_terms(short))
    back_pair = np.stack(two_terms(short.T / (devices * length)))
    long = forward.astype(ml_dtypes.bfloat16)
    longback = np.ascontiguousarray(forward.transpose(0, 2, 1)).astype(ml_dtypes.bfloat16)
    tail_rows = -(-3 * (feat_count - 1) // 8) * 8
    bf16, f32 = jnp.bfloat16, jnp.float32
    dma = pltpu.SemaphoreType.DMA
    anywhere = pl.BlockSpec(memory_space=pl.ANY)
    whole = pl.BlockSpec(memory_space=pltpu.VMEM)
    call = pl.pallas_call(
        functools.partial(kernel, devices, sections),
        out_shape=jax.ShapeDtypeStruct((length, channels), bf16),
        in_specs=[anywhere, whole, whole, anywhere, anywhere, anywhere, anywhere, anywhere],
        out_specs=whole,
        scratch_shapes=[
            pltpu.VMEM((3, length, channels), bf16),
            pltpu.VMEM(short_pair.shape, bf16),
            pltpu.VMEM(back_pair.shape, bf16),
            pltpu.VMEM(long.shape, bf16),
            pltpu.VMEM(longback.shape, bf16),
            pltpu.VMEM((tail_rows, channels), f32),
            pltpu.VMEM((tail_rows, channels), f32),
            pltpu.VMEM((devices, length, share), bf16),
            pltpu.VMEM((devices, length, share), f32),
            pltpu.VMEM((devices, length, share), f32),
            pltpu.VMEM((devices, length, share), bf16),
            pltpu.VMEM((devices, length, share), bf16),
            pltpu.VMEM((devices, length, share), f32),
            pltpu.VMEM((devices, length, share), f32),
            pltpu.VMEM((devices, 2 * length, share), bf16),
            pltpu.VMEM((devices, 2 * length, share), f32),
            pltpu.VMEM((devices, 2 * length, share), bf16),
            pltpu.VMEM((devices, length, share), bf16),
            pltpu.VMEM((devices, length, share), bf16),
            dma((6,)),
            dma((2,)),
            dma((devices,)),
            dma((devices,)),
            dma((devices,)),
            dma((devices,)),
            dma((4,)),
            dma((devices,)),
            dma((devices,)),
        ],
        compiler_params=pltpu.CompilerParams(has_side_effects=True, vmem_limit_bytes=48 * 1024 * 1024),
        name="mixer",
    )
    out = call(
        streams,
        taps,
        skip_gain,
        long_filter[0],
        jnp.asarray(short_pair),
        jnp.asarray(back_pair),
        jnp.asarray(long),
        jnp.asarray(longback),
    )
    return out[None]


def solution(mesh):
    devices, sections = mesh.shape["ctx"], mesh.shape["section"]

    def body(projected, feat_taps, skip_gain, long_filter):
        _, length, channels = long_filter.shape
        feat_count = feat_taps.shape[1]
        fits = channels % (128 * devices) == 0 and length % 128 == 0
        fits = fits and sections > 1 and devices > 1 and feat_count - 1 <= GROUP
        run = body_kernel if fits else body_plain
        return run(projected, feat_taps, skip_gain, long_filter)

    return jax.shard_map(
        body,
        mesh=mesh,
        in_specs=(
            P("section", "ctx", None, None),
            P("section", None, None, None),
            P("section", None),
            P("section", "ctx", None),
        ),
        out_specs=P("section", "ctx", None),
        check_vma=False,
    )
```

```python
import functools
import math

import jax
import jax.numpy as jnp
import ml_dtypes
import numpy as np
from jax import lax
from jax.experimental import pallas as pl
from jax.experimental.pallas import tpu as pltpu
from jax.sharding import PartitionSpec as P

GROUP = 16
MESH = pl.DeviceIdType.MESH


def tables(devices, length):
    total = devices * length
    r = np.arange(devices)
    p = np.arange(devices)
    s = np.arange(length)
    j = np.arange(length)
    short = np.exp(2j * np.pi * (((1 + 4 * r[:, None]) * p[None, :]) % (4 * devices)) / (4 * devices))
    phase = ((1 + 4 * r[:, None, None]) * j[None, None, :] + 4 * devices * s[None, :, None] * j[None, None, :]) % (4 * total)
    long = np.exp(2j * np.pi * phase / (4 * total))
    forward = np.concatenate(
        [np.concatenate([long.real, -long.imag], 2), np.concatenate([long.imag, long.real], 2)], 1
    )
    parts = np.stack([short.real, short.imag])
    return parts, forward


def two_terms(values):
    high = values.astype(ml_dtypes.bfloat16)
    low = (values - high.astype(np.float64)).astype(ml_dtypes.bfloat16)
    return high, low


def body_plain(projected, feat_taps, skip_gain, long_filter):
    devices = lax.axis_size("ctx")
    sections = lax.axis_size("section")
    streams = projected[0]
    length, _, channels = streams.shape
    share = channels // devices
    feat_count = feat_taps.shape[1]
    earlier = lax.ppermute(
        streams[length - (feat_count - 1) :], "ctx", [(i, i + 1) for i in range(devices - 1)]
    )
    extended = jnp.concatenate([earlier, streams], axis=0).astype(jnp.float32)
    featured = jnp.zeros((length, 3, channels), jnp.float32)
    for offset in range(feat_count):
        first = feat_count - 1 - offset
        featured = featured + feat_taps[0, offset].astype(jnp.float32) * extended[first : first + length]
    query = featured[:, 0]
    gated = featured[:, 1] * featured[:, 2]
    packed = jnp.stack([gated.astype(jnp.bfloat16), long_filter[0]])
    packed = packed.reshape(2, length, devices, share).transpose(2, 0, 1, 3)
    arrived = lax.all_to_all(packed, "ctx", split_axis=0, concat_axis=0, tiled=True)
    parts, forward = tables(devices, length)
    parts = jnp.asarray(parts, jnp.float32)
    forward = jnp.asarray(forward, jnp.float32)
    high = lax.Precision.HIGHEST
    blocks = arrived.astype(jnp.float32)
    partial = jnp.einsum("qrp,pkjc->krqjc", parts, blocks, precision=high)
    partial = partial.reshape(2, devices, 2 * length, share)
    spectrum = jnp.einsum("rxy,kryc->krxc", forward, partial, precision=high)
    data_re, data_im = spectrum[0, :, :length], spectrum[0, :, length:]
    filt_re, filt_im = spectrum[1, :, :length], spectrum[1, :, length:]
    product = jnp.concatenate(
        [data_re * filt_re - data_im * filt_im, data_re * filt_im + data_im * filt_re], 1
    )
    restored = jnp.einsum("rxy,rxc->ryc", forward, product, precision=high)
    restored = restored.reshape(devices, 2, length, share)
    conv = jnp.einsum("qrp,rqjc->pjc", parts, restored, precision=high) / (devices * length)
    back = lax.all_to_all(conv.astype(jnp.bfloat16), "ctx", split_axis=0, concat_axis=0, tiled=True)
    convolved = back.transpose(1, 0, 2).reshape(length, channels).astype(jnp.float32)
    output = (query * (convolved + skip_gain[0] * gated)).astype(jnp.bfloat16)
    return lax.ppermute(
        output[None], "section", [(i, (i + 1) % sections) for i in range(sections)]
    )


def partner(me, step, devices, arriving=False):
    if devices & (devices - 1) == 0:
        return me ^ step
    return lax.rem(me + (devices - step if arriving else step), devices)


def kernel(
    devices,
    sections,
    streams_ref,
    taps_ref,
    skip_ref,
    filter_ref,
    short_ref,
    back_ref,
    long_ref,
    longback_ref,
    out_ref,
    streams,
    taps_raw,
    taps,
    skip,
    short,
    back,
    long,
    longback,
    tail,
    halo,
    gated_out,
    query,
    skipped,
    filter_in,
    gated_in,
    query_in,
    skipped_in,
    partial,
    spectrum,
    restored,
    conv,
    conv_in,
    local_sem,
    halo_sem,
    filter_send,
    filter_recv,
    gated_send,
    gated_recv,
    cross_sem,
    conv_send,
    conv_recv,
):
    me = lax.axis_index("ctx")
    beyond = lax.rem(lax.axis_index("section") + 1, sections)
    length, channels = filter_ref.shape
    share = channels // devices
    feat_count = taps_ref.shape[0]
    keep = feat_count - 1
    rows = devices * GROUP

    def lanes(index):
        return pl.ds(pl.multiple_of(index * share, share), share)

    def filter_copy(step):
        to = partner(me, step, devices)
        return pltpu.make_async_remote_copy(
            src_ref=filter_ref.at[:, lanes(to)],
            dst_ref=filter_in.at[me],
            send_sem=filter_send.at[step],
            recv_sem=filter_recv.at[step],
            device_id={"ctx": to},
            device_id_type=MESH,
        )

    def gated_copy(step):
        to = partner(me, step, devices)
        return pltpu.make_async_remote_copy(
            src_ref=gated_out.at[to],
            dst_ref=gated_in.at[me],
            send_sem=gated_send.at[step],
            recv_sem=gated_recv.at[step],
            device_id={"ctx": to},
            device_id_type=MESH,
        )

    def conv_copy(step):
        to = partner(me, step, devices)
        return pltpu.make_async_remote_copy(
            src_ref=conv.at[to],
            dst_ref=conv_in.at[me],
            send_sem=conv_send.at[step],
            recv_sem=conv_recv.at[step],
            device_id={"ctx": to, "section": beyond},
            device_id_type=MESH,
        )

    def cross_copy(index, source, target):
        return pltpu.make_async_remote_copy(
            src_ref=source,
            dst_ref=target,
            send_sem=cross_sem.at[2 * index],
            recv_sem=cross_sem.at[2 * index + 1],
            device_id={"section": beyond},
            device_id_type=MESH,
        )

    halo_copy = pltpu.make_async_remote_copy(
        src_ref=tail,
        dst_ref=halo,
        send_sem=halo_sem.at[0],
        recv_sem=halo_sem.at[1],
        device_id={"ctx": lax.rem(me + 1, devices)},
        device_id_type=MESH,
    )
    load_streams = pltpu.make_async_copy(streams_ref, streams, local_sem.at[0])
    own_filter = pltpu.make_async_copy(filter_ref.at[:, lanes(me)], filter_in.at[me], local_sem.at[1])
    loads = [
        pltpu.make_async_copy(source, target, local_sem.at[2 + i])
        for i, (source, target) in enumerate(
            [(short_ref, short), (long_ref, long), (longback_ref, longback), (back_ref, back)]
        )
    ]
    load_taps = pltpu.make_async_copy(taps_ref, taps_raw, local_sem.at[6])
    load_skip = pltpu.make_async_copy(skip_ref, skip, local_sem.at[7])

    barrier = pltpu.get_barrier_semaphore()
    before = lax.rem(lax.axis_index("section") + sections - 1, sections)
    others = [beyond] if sections == 2 else [beyond, before]

    @pl.loop(1, devices)
    def _(step):
        pl.semaphore_signal(
            barrier, inc=1, device_id={"ctx": lax.rem(me + step, devices)}, device_id_type=MESH
        )

    for other in others:

        @pl.loop(0, devices)
        def _(step):
            pl.semaphore_signal(
                barrier,
                inc=1,
                device_id={"ctx": lax.rem(me + step, devices), "section": other},
                device_id_type=MESH,
            )

    load_streams.start()
    load_taps.start()
    load_skip.start()
    pl.semaphore_wait(barrier, devices - 1 + len(others) * devices)
    ahead = min(3, devices - 1)

    @pl.loop(0, ahead)
    def _(i):
        filter_copy(1 + i).start()

    load_streams.wait()

    for stream in range(3):
        last = streams[stream, length - GROUP :, :].astype(jnp.float32)
        tail[stream * keep : (stream + 1) * keep, :] = last[GROUP - keep :, :]
    if tail.shape[0] > 3 * keep:
        tail[3 * keep :, :] = jnp.zeros((tail.shape[0] - 3 * keep, channels), jnp.float32)

    @pl.when(me < devices - 1)
    def _():
        halo_copy.start()

    @pl.loop(ahead, devices - 1)
    def _(i):
        filter_copy(1 + i).start()

    own_filter.start()
    for copy in loads:
        copy.start()
    load_taps.wait()
    load_skip.wait()
    for offset in range(feat_count):
        taps[offset] = taps_raw[offset].astype(jnp.float32)

    @pl.when(me > 0)
    def _():
        halo_copy.wait_recv()

    @pl.when(me == 0)
    def _():
        halo[...] = jnp.zeros_like(halo)

    row_ids = lax.broadcasted_iota(jnp.int32, (length, share), 0)

    def features(index):
        at = lanes(index)
        found = []
        for stream in range(3):
            values = streams[stream, :, at].astype(jnp.float32)
            total = taps[0, pl.ds(stream, 1), at] * values
            for offset in range(1, feat_count):
                moved = pltpu.roll(values, offset, 0)
                for row in range(offset):
                    before = halo[pl.ds(stream * keep + keep - offset + row, 1), at]
                    moved = jnp.where(row_ids == row, before, moved)
                total = total + taps[offset, pl.ds(stream, 1), at] * moved
            found.append(total)
        gated = found[1] * found[2]
        gated_out[index] = gated.astype(jnp.bfloat16)
        query[index] = found[0]
        skipped[index] = skip[:, at] * gated

    @pl.loop(0, devices - 1)
    def _(i):
        step = 1 + i
        features(partner(me, step, devices))
        gated_copy(step).start()

    features(me)
    gated_in[me] = gated_out[me]
    cross_copy(0, query, query_in).start()
    cross_copy(1, skipped, skipped_in).start()

    def group(g, first=0):
        start = first + g * GROUP
        return pl.ds(start if isinstance(start, int) else pl.multiple_of(start, GROUP), GROUP)

    def two_dots(table, values):
        done = jnp.dot(table[0], values, preferred_element_type=jnp.float32)
        return done + jnp.dot(table[1], values, preferred_element_type=jnp.float32)

    def short_transform(arrived):
        @pl.loop(0, length // GROUP, step=2, unroll=length // (2 * GROUP))
        def _(g):
            values = [arrived[:, group(g + i), :].reshape(rows, share) for i in range(2)]
            done = two_dots(short, jnp.concatenate(values, 1)).astype(jnp.bfloat16)
            for i in range(2):
                part = done[:, i * share : (i + 1) * share].reshape(2, devices, GROUP, share)
                partial[:, group(g + i), :] = part[0]
                partial[:, group(g + i, length), :] = part[1]

    own_filter.wait()

    @pl.loop(0, devices - 1)
    def _(i):
        filter_copy(1 + i).wait_recv()

    for copy in loads:
        copy.wait()
    short_transform(filter_in)

    @pl.loop(0, devices, unroll=devices)
    def _(r):
        spectrum[r] = jnp.dot(long[r], partial[r], preferred_element_type=jnp.float32)

    @pl.loop(0, devices - 1)
    def _(i):
        gated_copy(1 + i).wait_recv()

    short_transform(gated_in)

    @pl.loop(0, devices, unroll=devices)
    def _(r):
        data = jnp.dot(long[r], partial[r], preferred_element_type=jnp.float32)
        data_re, data_im = data[:length], data[length:]
        filt_re, filt_im = spectrum[r, :length], spectrum[r, length:]
        product = jnp.concatenate(
            [data_re * filt_re - data_im * filt_im, data_re * filt_im + data_im * filt_re], 0
        )
        restored[r] = jnp.dot(
            longback[r], product.astype(jnp.bfloat16), preferred_element_type=jnp.float32
        ).astype(jnp.bfloat16)

    @pl.loop(0, length // GROUP, step=2, unroll=length // (2 * GROUP))
    def _(g):
        values = [
            jnp.concatenate(
                [restored[:, group(g + i, first), :].reshape(rows, share) for first in (0, length)], 0
            )
            for i in range(2)
        ]
        done = two_dots(back, jnp.concatenate(values, 1)).astype(jnp.bfloat16)
        for i in range(2):
            conv[:, group(g + i), :] = done[:, i * share : (i + 1) * share].reshape(devices, GROUP, share)

    @pl.loop(1, devices)
    def _(step):
        conv_copy(step).start()

    conv_copy(0).start()

    cross_copy(0, query, query_in).wait()
    cross_copy(1, skipped, skipped_in).wait()

    @pl.when(me < devices - 1)
    def _():
        halo_copy.wait_send()

    @pl.loop(0, devices - 1)
    def _(i):
        filter_copy(1 + i).wait_send()
        gated_copy(1 + i).wait_send()

    @pl.loop(0, devices)
    def _(i):
        step = lax.rem(i + 1, devices)
        conv_copy(step).wait_recv()
        source = partner(me, step, devices, arriving=True)
        mixed = query_in[source] * (conv_in[source].astype(jnp.float32) + skipped_in[source])
        out_ref[:, lanes(source)] = mixed.astype(jnp.bfloat16)

    @pl.loop(0, devices)
    def _(i):
        conv_copy(i).wait_send()


def body_kernel(projected, feat_taps, skip_gain, long_filter):
    devices = lax.axis_size("ctx")
    sections = lax.axis_size("section")
    streams = jnp.transpose(projected[0], (1, 0, 2))
    _, length, channels = streams.shape
    share = channels // devices
    feat_count = feat_taps.shape[1]
    parts, forward = tables(devices, length)
    eye = np.eye(GROUP)
    short = np.einsum("qrp,ab->qrapb", parts, eye).reshape(2 * devices * GROUP, devices * GROUP)
    short_pair = np.stack(two_terms(short))
    back_pair = np.stack(two_terms(short.T / (devices * length)))
    long = forward.astype(ml_dtypes.bfloat16)
    longback = np.ascontiguousarray(forward.transpose(0, 2, 1)).astype(ml_dtypes.bfloat16)
    tail_rows = -(-3 * (feat_count - 1) // 8) * 8
    bf16, f32 = jnp.bfloat16, jnp.float32
    dma = pltpu.SemaphoreType.DMA
    stays = pl.BlockSpec(memory_space=pltpu.HBM)
    whole = pl.BlockSpec(memory_space=pltpu.VMEM)
    call = pl.pallas_call(
        functools.partial(kernel, devices, sections),
        out_shape=jax.ShapeDtypeStruct((length, channels), bf16),
        in_specs=[stays] * 8,
        out_specs=whole,
        scratch_shapes=[
            pltpu.VMEM((3, length, channels), bf16),
            pltpu.VMEM((feat_count, 3, channels), bf16),
            pltpu.VMEM((feat_count, 3, channels), f32),
            pltpu.VMEM((1, channels), f32),
            pltpu.VMEM(short_pair.shape, bf16),
            pltpu.VMEM(back_pair.shape, bf16),
            pltpu.VMEM(long.shape, bf16),
            pltpu.VMEM(longback.shape, bf16),
            pltpu.VMEM((tail_rows, channels), f32),
            pltpu.VMEM((tail_rows, channels), f32),
            pltpu.VMEM((devices, length, share), bf16),
            pltpu.VMEM((devices, length, share), f32),
            pltpu.VMEM((devices, length, share), f32),
            pltpu.VMEM((devices, length, share), bf16),
            pltpu.VMEM((devices, length, share), bf16),
            pltpu.VMEM((devices, length, share), f32),
            pltpu.VMEM((devices, length, share), f32),
            pltpu.VMEM((devices, 2 * length, share), bf16),
            pltpu.VMEM((devices, 2 * length, share), f32),
            pltpu.VMEM((devices, 2 * length, share), bf16),
            pltpu.VMEM((devices, length, share), bf16),
            pltpu.VMEM((devices, length, share), bf16),
            dma((8,)),
            dma((2,)),
            dma((devices,)),
            dma((devices,)),
            dma((devices,)),
            dma((devices,)),
            dma((4,)),
            dma((devices,)),
            dma((devices,)),
        ],
        compiler_params=pltpu.CompilerParams(collective_id=0, has_side_effects=True, vmem_limit_bytes=127 * 512 * 1024),
        name="mixer",
    )
    out = call(
        streams,
        feat_taps[0],
        skip_gain,
        long_filter[0],
        jnp.asarray(short_pair),
        jnp.asarray(back_pair),
        jnp.asarray(long),
        jnp.asarray(longback),
    )
    return out[None]


def solution(mesh):
    devices, sections = mesh.shape["ctx"], mesh.shape["section"]

    def body(projected, feat_taps, skip_gain, long_filter):
        _, length, channels = long_filter.shape
        feat_count = feat_taps.shape[1]
        fits = channels % (128 * devices) == 0 and length % 128 == 0
        fits = fits and sections > 1 and devices > 1 and feat_count - 1 <= GROUP
        run = body_kernel if fits else body_plain
        return run(projected, feat_taps, skip_gain, long_filter)

    return jax.shard_map(
        body,
        mesh=mesh,
        in_specs=(
            P("section", "ctx", None, None),
            P("section", None, None, None),
            P("section", None),
            P("section", "ctx", None),
        ),
        out_specs=P("section", "ctx", None),
        check_vma=False,
    )
```

```python
import functools
import math

import jax
import jax.numpy as jnp
import ml_dtypes
import numpy as np
from jax import lax
from jax.experimental import pallas as pl
from jax.experimental.pallas import tpu as pltpu
from jax.sharding import PartitionSpec as P

GROUP = 16
MESH = pl.DeviceIdType.MESH


def tables(devices, length):
    total = devices * length
    r = np.arange(devices)
    p = np.arange(devices)
    s = np.arange(length)
    j = np.arange(length)
    short = np.exp(2j * np.pi * (((1 + 4 * r[:, None]) * p[None, :]) % (4 * devices)) / (4 * devices))
    phase = ((1 + 4 * r[:, None, None]) * j[None, None, :] + 4 * devices * s[None, :, None] * j[None, None, :]) % (4 * total)
    long = np.exp(2j * np.pi * phase / (4 * total))
    forward = np.concatenate(
        [np.concatenate([long.real, -long.imag], 2), np.concatenate([long.imag, long.real], 2)], 1
    )
    parts = np.stack([short.real, short.imag])
    return parts, forward


def two_terms(values):
    high = values.astype(ml_dtypes.bfloat16)
    low = (values - high.astype(np.float64)).astype(ml_dtypes.bfloat16)
    return high, low


def body_plain(projected, feat_taps, skip_gain, long_filter):
    devices = lax.axis_size("ctx")
    sections = lax.axis_size("section")
    streams = projected[0]
    length, _, channels = streams.shape
    share = channels // devices
    feat_count = feat_taps.shape[1]
    earlier = lax.ppermute(
        streams[length - (feat_count - 1) :], "ctx", [(i, i + 1) for i in range(devices - 1)]
    )
    extended = jnp.concatenate([earlier, streams], axis=0).astype(jnp.float32)
    featured = jnp.zeros((length, 3, channels), jnp.float32)
    for offset in range(feat_count):
        first = feat_count - 1 - offset
        featured = featured + feat_taps[0, offset].astype(jnp.float32) * extended[first : first + length]
    query = featured[:, 0]
    gated = featured[:, 1] * featured[:, 2]
    packed = jnp.stack([gated.astype(jnp.bfloat16), long_filter[0]])
    packed = packed.reshape(2, length, devices, share).transpose(2, 0, 1, 3)
    arrived = lax.all_to_all(packed, "ctx", split_axis=0, concat_axis=0, tiled=True)
    parts, forward = tables(devices, length)
    parts = jnp.asarray(parts, jnp.float32)
    forward = jnp.asarray(forward, jnp.float32)
    high = lax.Precision.HIGHEST
    blocks = arrived.astype(jnp.float32)
    partial = jnp.einsum("qrp,pkjc->krqjc", parts, blocks, precision=high)
    partial = partial.reshape(2, devices, 2 * length, share)
    spectrum = jnp.einsum("rxy,kryc->krxc", forward, partial, precision=high)
    data_re, data_im = spectrum[0, :, :length], spectrum[0, :, length:]
    filt_re, filt_im = spectrum[1, :, :length], spectrum[1, :, length:]
    product = jnp.concatenate(
        [data_re * filt_re - data_im * filt_im, data_re * filt_im + data_im * filt_re], 1
    )
    restored = jnp.einsum("rxy,rxc->ryc", forward, product, precision=high)
    restored = restored.reshape(devices, 2, length, share)
    conv = jnp.einsum("qrp,rqjc->pjc", parts, restored, precision=high) / (devices * length)
    back = lax.all_to_all(conv.astype(jnp.bfloat16), "ctx", split_axis=0, concat_axis=0, tiled=True)
    convolved = back.transpose(1, 0, 2).reshape(length, channels).astype(jnp.float32)
    output = (query * (convolved + skip_gain[0] * gated)).astype(jnp.bfloat16)
    return lax.ppermute(
        output[None], "section", [(i, (i + 1) % sections) for i in range(sections)]
    )


def partner(me, step, devices, arriving=False):
    if devices & (devices - 1) == 0:
        return me ^ step
    return lax.rem(me + (devices - step if arriving else step), devices)


def bit_sum(value, devices):
    total, size = value, 1
    while 1 << size < devices:
        total = total ^ (value >> size)
        size += 1
    return total & 1


def early_first(me, i, devices):
    if devices & (devices - 1) != 0:
        return i
    half = devices // 2
    place = lax.rem(i, half)
    late = i // half
    return 2 * place + (bit_sum(place, devices) ^ bit_sum(me, devices) ^ late)


def kernel(
    devices,
    sections,
    streams_ref,
    taps_ref,
    skip_ref,
    filter_ref,
    short_ref,
    back_ref,
    long_ref,
    longback_ref,
    out_ref,
    streams,
    taps_raw,
    taps,
    skip,
    short,
    back,
    long,
    longback,
    tail,
    halo,
    gated_out,
    query,
    skipped,
    filter_in,
    gated_in,
    query_in,
    skipped_in,
    partial,
    spectrum,
    restored,
    conv,
    conv_in,
    local_sem,
    halo_sem,
    filter_send,
    filter_recv,
    gated_send,
    gated_recv,
    cross_sem,
    conv_send,
    conv_recv,
):
    me = lax.axis_index("ctx")
    beyond = lax.rem(lax.axis_index("section") + 1, sections)
    length, channels = filter_ref.shape
    share = channels // devices
    feat_count = taps_ref.shape[0]
    keep = feat_count - 1
    rows = devices * GROUP

    def lanes(index):
        return pl.ds(pl.multiple_of(index * share, share), share)

    def filter_copy(step):
        to = partner(me, step, devices)
        return pltpu.make_async_remote_copy(
            src_ref=filter_ref.at[:, lanes(to)],
            dst_ref=filter_in.at[me],
            send_sem=filter_send.at[step],
            recv_sem=filter_recv.at[step],
            device_id={"ctx": to},
            device_id_type=MESH,
        )

    def gated_copy(step):
        to = partner(me, step, devices)
        return pltpu.make_async_remote_copy(
            src_ref=gated_out.at[to],
            dst_ref=gated_in.at[me],
            send_sem=gated_send.at[step],
            recv_sem=gated_recv.at[step],
            device_id={"ctx": to},
            device_id_type=MESH,
        )

    def conv_copy(step):
        to = partner(me, step, devices)
        return pltpu.make_async_remote_copy(
            src_ref=conv.at[to],
            dst_ref=conv_in.at[me],
            send_sem=conv_send.at[step],
            recv_sem=conv_recv.at[step],
            device_id={"ctx": to, "section": beyond},
            device_id_type=MESH,
        )

    def cross_copy(index, source, target):
        return pltpu.make_async_remote_copy(
            src_ref=source,
            dst_ref=target,
            send_sem=cross_sem.at[2 * index],
            recv_sem=cross_sem.at[2 * index + 1],
            device_id={"section": beyond},
            device_id_type=MESH,
        )

    halo_copy = pltpu.make_async_remote_copy(
        src_ref=tail,
        dst_ref=halo,
        send_sem=halo_sem.at[0],
        recv_sem=halo_sem.at[1],
        device_id={"ctx": lax.rem(me + 1, devices)},
        device_id_type=MESH,
    )
    load_streams = pltpu.make_async_copy(streams_ref, streams, local_sem.at[0])
    own_filter = pltpu.make_async_copy(filter_ref.at[:, lanes(me)], filter_in.at[me], local_sem.at[1])
    loads = [
        pltpu.make_async_copy(source, target, local_sem.at[2 + i])
        for i, (source, target) in enumerate(
            [(short_ref, short), (long_ref, long), (longback_ref, longback), (back_ref, back)]
        )
    ]
    load_taps = pltpu.make_async_copy(taps_ref, taps_raw, local_sem.at[6])
    load_skip = pltpu.make_async_copy(skip_ref, skip, local_sem.at[7])

    barrier = pltpu.get_barrier_semaphore()
    before = lax.rem(lax.axis_index("section") + sections - 1, sections)
    others = [beyond] if sections == 2 else [beyond, before]

    @pl.loop(1, devices)
    def _(step):
        pl.semaphore_signal(
            barrier, inc=1, device_id={"ctx": lax.rem(me + step, devices)}, device_id_type=MESH
        )

    for other in others:

        @pl.loop(0, devices)
        def _(step):
            pl.semaphore_signal(
                barrier,
                inc=1,
                device_id={"ctx": lax.rem(me + step, devices), "section": other},
                device_id_type=MESH,
            )

    load_streams.start()
    load_taps.start()
    load_skip.start()
    pl.semaphore_wait(barrier, devices - 1 + len(others) * devices)
    ahead = min(3, devices - 1)

    def filter_start(i):
        step = early_first(me, i, devices)

        @pl.when(step > 0)
        def _():
            filter_copy(step).start()

    @pl.loop(0, ahead)
    def _(i):
        filter_start(i)

    load_streams.wait()

    for stream in range(3):
        last = streams[stream, length - GROUP :, :].astype(jnp.float32)
        tail[stream * keep : (stream + 1) * keep, :] = last[GROUP - keep :, :]
    if tail.shape[0] > 3 * keep:
        tail[3 * keep :, :] = jnp.zeros((tail.shape[0] - 3 * keep, channels), jnp.float32)

    @pl.when(me < devices - 1)
    def _():
        halo_copy.start()

    @pl.loop(ahead, devices)
    def _(i):
        filter_start(i)

    own_filter.start()
    for copy in loads:
        copy.start()
    load_taps.wait()
    load_skip.wait()
    for offset in range(feat_count):
        taps[offset] = taps_raw[offset].astype(jnp.float32)

    @pl.when(me > 0)
    def _():
        halo_copy.wait_recv()

    @pl.when(me == 0)
    def _():
        halo[...] = jnp.zeros_like(halo)

    row_ids = lax.broadcasted_iota(jnp.int32, (length, share), 0)

    def features(index):
        at = lanes(index)
        found = []
        for stream in range(3):
            values = streams[stream, :, at].astype(jnp.float32)
            total = taps[0, pl.ds(stream, 1), at] * values
            for offset in range(1, feat_count):
                moved = pltpu.roll(values, offset, 0)
                for row in range(offset):
                    before = halo[pl.ds(stream * keep + keep - offset + row, 1), at]
                    moved = jnp.where(row_ids == row, before, moved)
                total = total + taps[offset, pl.ds(stream, 1), at] * moved
            found.append(total)
        gated = found[1] * found[2]
        gated_out[index] = gated.astype(jnp.bfloat16)
        query[index] = found[0]
        skipped[index] = skip[:, at] * gated

    @pl.loop(0, devices)
    def _(i):
        step = early_first(me, i, devices)
        features(partner(me, step, devices))

        @pl.when(step > 0)
        def _():
            gated_copy(step).start()

    gated_in[me] = gated_out[me]
    cross_copy(0, query, query_in).start()
    cross_copy(1, skipped, skipped_in).start()

    def group(g, first=0):
        start = first + g * GROUP
        return pl.ds(start if isinstance(start, int) else pl.multiple_of(start, GROUP), GROUP)

    def two_dots(table, values):
        done = jnp.dot(table[0], values, preferred_element_type=jnp.float32)
        return done + jnp.dot(table[1], values, preferred_element_type=jnp.float32)

    def short_transform(arrived):
        @pl.loop(0, length // GROUP, step=2, unroll=length // (2 * GROUP))
        def _(g):
            values = [arrived[:, group(g + i), :].reshape(rows, share) for i in range(2)]
            done = two_dots(short, jnp.concatenate(values, 1)).astype(jnp.bfloat16)
            for i in range(2):
                part = done[:, i * share : (i + 1) * share].reshape(2, devices, GROUP, share)
                partial[:, group(g + i), :] = part[0]
                partial[:, group(g + i, length), :] = part[1]

    own_filter.wait()

    @pl.loop(0, devices - 1)
    def _(i):
        filter_copy(1 + i).wait_recv()

    for copy in loads:
        copy.wait()
    short_transform(filter_in)

    @pl.loop(0, devices, unroll=devices)
    def _(r):
        spectrum[r] = jnp.dot(long[r], partial[r], preferred_element_type=jnp.float32)

    @pl.loop(0, devices - 1)
    def _(i):
        gated_copy(1 + i).wait_recv()

    short_transform(gated_in)

    @pl.loop(0, devices, unroll=devices)
    def _(r):
        data = jnp.dot(long[r], partial[r], preferred_element_type=jnp.float32)
        data_re, data_im = data[:length], data[length:]
        filt_re, filt_im = spectrum[r, :length], spectrum[r, length:]
        product = jnp.concatenate(
            [data_re * filt_re - data_im * filt_im, data_re * filt_im + data_im * filt_re], 0
        )
        restored[r] = jnp.dot(
            longback[r], product.astype(jnp.bfloat16), preferred_element_type=jnp.float32
        ).astype(jnp.bfloat16)

    @pl.loop(0, length // GROUP, step=2, unroll=length // (2 * GROUP))
    def _(g):
        values = [
            jnp.concatenate(
                [restored[:, group(g + i, first), :].reshape(rows, share) for first in (0, length)], 0
            )
            for i in range(2)
        ]
        done = two_dots(back, jnp.concatenate(values, 1)).astype(jnp.bfloat16)
        for i in range(2):
            conv[:, group(g + i), :] = done[:, i * share : (i + 1) * share].reshape(devices, GROUP, share)

    @pl.loop(0, devices)
    def _(step):
        conv_copy(devices - 1 - step).start()


    cross_copy(0, query, query_in).wait()
    cross_copy(1, skipped, skipped_in).wait()

    @pl.when(me < devices - 1)
    def _():
        halo_copy.wait_send()

    @pl.loop(0, devices - 1)
    def _(i):
        filter_copy(1 + i).wait_send()
        gated_copy(1 + i).wait_send()

    @pl.loop(0, devices)
    def _(i):
        step = lax.rem(i + 1, devices)
        conv_copy(step).wait_recv()
        source = partner(me, step, devices, arriving=True)
        mixed = query_in[source] * (conv_in[source].astype(jnp.float32) + skipped_in[source])
        out_ref[:, lanes(source)] = mixed.astype(jnp.bfloat16)

    @pl.loop(0, devices)
    def _(i):
        conv_copy(i).wait_send()


def body_kernel(projected, feat_taps, skip_gain, long_filter):
    devices = lax.axis_size("ctx")
    sections = lax.axis_size("section")
    streams = jnp.transpose(projected[0], (1, 0, 2))
    _, length, channels = streams.shape
    share = channels // devices
    feat_count = feat_taps.shape[1]
    parts, forward = tables(devices, length)
    eye = np.eye(GROUP)
    short = np.einsum("qrp,ab->qrapb", parts, eye).reshape(2 * devices * GROUP, devices * GROUP)
    short_pair = np.stack(two_terms(short))
    back_pair = np.stack(two_terms(short.T / (devices * length)))
    long = forward.astype(ml_dtypes.bfloat16)
    longback = np.ascontiguousarray(forward.transpose(0, 2, 1)).astype(ml_dtypes.bfloat16)
    tail_rows = -(-3 * (feat_count - 1) // 8) * 8
    bf16, f32 = jnp.bfloat16, jnp.float32
    dma = pltpu.SemaphoreType.DMA
    stays = pl.BlockSpec(memory_space=pltpu.HBM)
    whole = pl.BlockSpec(memory_space=pltpu.VMEM)
    call = pl.pallas_call(
        functools.partial(kernel, devices, sections),
        out_shape=jax.ShapeDtypeStruct((length, channels), bf16),
        in_specs=[stays] * 8,
        out_specs=whole,
        scratch_shapes=[
            pltpu.VMEM((3, length, channels), bf16),
            pltpu.VMEM((feat_count, 3, channels), bf16),
            pltpu.VMEM((feat_count, 3, channels), f32),
            pltpu.VMEM((1, channels), f32),
            pltpu.VMEM(short_pair.shape, bf16),
            pltpu.VMEM(back_pair.shape, bf16),
            pltpu.VMEM(long.shape, bf16),
            pltpu.VMEM(longback.shape, bf16),
            pltpu.VMEM((tail_rows, channels), f32),
            pltpu.VMEM((tail_rows, channels), f32),
            pltpu.VMEM((devices, length, share), bf16),
            pltpu.VMEM((devices, length, share), f32),
            pltpu.VMEM((devices, length, share), f32),
            pltpu.VMEM((devices, length, share), bf16),
            pltpu.VMEM((devices, length, share), bf16),
            pltpu.VMEM((devices, length, share), f32),
            pltpu.VMEM((devices, length, share), f32),
            pltpu.VMEM((devices, 2 * length, share), bf16),
            pltpu.VMEM((devices, 2 * length, share), f32),
            pltpu.VMEM((devices, 2 * length, share), bf16),
            pltpu.VMEM((devices, length, share), bf16),
            pltpu.VMEM((devices, length, share), bf16),
            dma((8,)),
            dma((2,)),
            dma((devices,)),
            dma((devices,)),
            dma((devices,)),
            dma((devices,)),
            dma((4,)),
            dma((devices,)),
            dma((devices,)),
        ],
        compiler_params=pltpu.CompilerParams(collective_id=0, has_side_effects=True, vmem_limit_bytes=127 * 512 * 1024),
        name="mixer",
    )
    out = call(
        streams,
        feat_taps[0],
        skip_gain,
        long_filter[0],
        jnp.asarray(short_pair),
        jnp.asarray(back_pair),
        jnp.asarray(long),
        jnp.asarray(longback),
    )
    return out[None]


def solution(mesh):
    devices, sections = mesh.shape["ctx"], mesh.shape["section"]

    def body(projected, feat_taps, skip_gain, long_filter):
        _, length, channels = long_filter.shape
        feat_count = feat_taps.shape[1]
        fits = channels % (128 * devices) == 0 and length % 128 == 0
        fits = fits and sections > 1 and devices > 1 and feat_count - 1 <= GROUP
        run = body_kernel if fits else body_plain
        return run(projected, feat_taps, skip_gain, long_filter)

    return jax.shard_map(
        body,
        mesh=mesh,
        in_specs=(
            P("section", "ctx", None, None),
            P("section", None, None, None),
            P("section", None),
            P("section", "ctx", None),
        ),
        out_specs=P("section", "ctx", None),
        check_vma=False,
    )
```
